512 devices in a mesh: seq: 64 (over x, z), head: 8 (over y, core).
Axes of the slice: x: 4, y: 4, z: 16, core: 2. Of those that a mesh axis runs over, the one named last changes fastest.
Arguments:
- queries: bfloat16 [256, 8192], P('seq', 'head'), may hold values from -8 to 8
- doc_kv: bfloat16 [2, 131072, 1024], P(None, 'seq', 'head'), may hold values from -4 to 4
- leaf_kv: bfloat16 [2, 65536, 1024], P(None, 'seq', 'head'), may hold values from -4 to 4
- suffix_kv: bfloat16 [2, 256, 512, 1024], P(None, 'seq', None, 'head'), may hold values from -4 to 4
- suffix_len: int32 [256], P('seq'), may hold values from 1 to 512, as said below
- parent: int32 [64], replicated, may hold values from 0 to 15, as said below
- row_leaf: int32 [256], replicated, may hold values from 0 to 63, as said below
- out_weight: bfloat16 [8192, 8192], P('head', 'seq'), may hold values from -0.25 to 0.25
Outputs:
- layer_out: bfloat16 [256, 8192], P('head', 'seq')
The draws below stay inside these ranges and needn't reach their ends.
Inputs may be any that keep to these rules, and one draw needn't show every extreme that they name: Every document is the parent of exactly 4 second-level nodes. `row_leaf`: at most 12 rows have the same second-level node; every node of one document has exactly 12. `suffix_len`: some row has all 512 suffix tokens live.
All inputs are finite; a program needn't handle non-finite values.
Results may differ from the reference program's by a relative error of at most 0.0052.
Values may be sent and summed in bfloat16 or wider, within the bound.
A program may use at most 64 MiB of HBM per device.

```python
import jax
import jax.numpy as jnp
from jax import lax

QH = 64
KVH = 8
HD = 128
D = 8192
NODES1 = 16
LEN1 = 8192
LEN2 = 1024
SUF = 512
LEAF_MOST = 12
NODES2 = 64
ROWS = 256


def tree_links(key):
    folded = jax.random.fold_in(key, 501)
    k_parent, k_favoured, k_slots, k_rows = jax.random.split(folded, 4)
    parent = (jax.random.permutation(k_parent, NODES2) % NODES1).astype(jnp.int32)
    favoured_doc = jax.random.randint(k_favoured, (), 0, NODES1)
    slot_count = NODES2 * LEAF_MOST
    slot_leaf = jnp.arange(slot_count, dtype=jnp.int32) // LEAF_MOST
    favoured = parent[slot_leaf] == favoured_doc
    shuffled = jax.random.permutation(k_slots, slot_count).astype(jnp.int32)
    ranking = jnp.where(favoured, shuffled - slot_count, shuffled)
    chosen = jnp.argsort(ranking)[:ROWS]
    leaves = (chosen // LEAF_MOST).astype(jnp.int32)
    return (parent, leaves[jax.random.permutation(k_rows, ROWS)])


def draw_parent(key, part):
    tree_pair = tree_links(key)
    return tree_pair[0]


def draw_row_leaf(key, part):
    tree_pair = tree_links(key)
    return tree_pair[1]


def draw_suffix_len(key, part):
    key = jax.random.fold_in(key, 3)
    k_len, k_pos = jax.random.split(key)
    lengths = jax.random.randint(k_len, (ROWS,), 1, SUF + 1)
    longest = jax.random.randint(k_pos, (), 0, ROWS)
    return jnp.where(jnp.arange(ROWS) == longest, SUF, lengths).astype(jnp.int32)


def draw_queries(key, part):
    key = jax.random.fold_in(key, 4)
    return jnp.clip(2.5 * jax.random.normal(key, (ROWS, QH * HD), jnp.float32), -8.0, 8.0).astype(jnp.bfloat16)


def draw_doc_kv(key, part):
    key = jax.random.fold_in(key, 5)
    token_total = NODES1 * LEN1
    return jnp.clip(jax.random.normal(key, (2, token_total, KVH * HD), jnp.float32), -4.0, 4.0).astype(jnp.bfloat16)


def steps_of(stream_key, extent, cuts, low, largest):
    level = 1.0
    for axis_at, parts in cuts:
        steps = jax.random.uniform(jax.random.fold_in(jax.random.fold_in(stream_key, 6), axis_at), (parts,), jnp.float32, low / len(cuts), largest / len(cuts))
        level = level * jnp.repeat(jnp.exp(steps), extent[axis_at] // parts).reshape((-1,) + (1,) * (len(extent) - 1 - axis_at))
    return level


def scatter_about(stream_key, shape, spread, reach, cuts=(), kind=jnp.bfloat16):
    result = spread * jax.random.normal(stream_key, shape, jnp.float32)
    if cuts:
        result = result * steps_of(stream_key, shape, cuts, -0.22, 0.18)
    return jnp.clip(result, -reach, reach).astype(kind)


def setup_inputs(seed: int = 0) -> dict:
    splits = jax.random.split(jax.random.key(seed), 9)
    queries = draw_queries(jax.random.fold_in(splits[8], 71), 0)
    doc_kv = draw_doc_kv(jax.random.fold_in(splits[8], 71), 0)
    leaf_kv = scatter_about(splits[2], (2, NODES2 * LEN2, KVH * HD), 1.0, 4.0, ((1, 64), (2, 8)))
    suffix_kv = scatter_about(splits[3], (2, ROWS, SUF, KVH * HD), 1.0, 4.0, ((1, 64), (3, 8)))
    suffix_len = draw_suffix_len(jax.random.fold_in(splits[8], 71), 0)
    parent = draw_parent(jax.random.fold_in(splits[8], 71), 0)
    row_leaf = draw_row_leaf(jax.random.fold_in(splits[8], 71), 0)
    out_weight = scatter_about(splits[7], (QH * HD, D), (QH * HD // 16) ** -0.5, 0.25, ((0, 8), (1, 64)))
    return dict(queries=queries, doc_kv=doc_kv, leaf_kv=leaf_kv, suffix_kv=suffix_kv, suffix_len=suffix_len, parent=parent, row_leaf=row_leaf, out_weight=out_weight)


NEG_FILL = -1.0e30


def reference(queries, doc_kv, leaf_kv, suffix_kv, suffix_len, parent, row_leaf, out_weight):
    group_size = QH // KVH
    scaling = HD ** -0.5
    zero_index = jnp.zeros((), jnp.int32)

    def per_row(row_index):
        leaf_node = row_leaf[row_index].astype(jnp.int32)
        document = parent[leaf_node].astype(jnp.int32)
        doc_part = lax.dynamic_slice(doc_kv, (zero_index, (document * LEN1).astype(jnp.int32), zero_index), (2, LEN1, KVH * HD))
        leaf_part = lax.dynamic_slice(leaf_kv, (zero_index, (leaf_node * LEN2).astype(jnp.int32), zero_index), (2, LEN2, KVH * HD))
        own_part = lax.dynamic_index_in_dim(suffix_kv, row_index, 1, keepdims=False)
        context = jnp.concatenate([doc_part, leaf_part, own_part], axis=1).astype(jnp.float32)
        context = context.reshape(2, LEN1 + LEN2 + SUF, KVH, HD)
        usable = jnp.concatenate([jnp.ones((LEN1 + LEN2,), dtype=bool), jnp.arange(SUF) < suffix_len[row_index]])
        query_vec = queries[row_index].astype(jnp.float32).reshape(KVH, group_size, HD)
        scores = jnp.einsum("kgh,tkh->kgt", query_vec, context[0]) * scaling
        scores = jnp.where(usable[None, None, :], scores, NEG_FILL)
        row_top = jnp.max(scores, axis=-1, keepdims=True)
        weights = jnp.exp(scores - row_top)
        totals = jnp.sum(weights, axis=-1)
        rounded = lax.optimization_barrier(weights.astype(jnp.bfloat16)).astype(jnp.float32)
        accum = jnp.einsum("kgt,tkh->kgh", rounded, context[1])
        return (accum / totals[..., None]).reshape(QH * HD).astype(jnp.bfloat16)

    attention = lax.map(per_row, jnp.arange(ROWS, dtype=jnp.int32))
    return jnp.dot(attention, out_weight, preferred_element_type=jnp.float32).astype(jnp.bfloat16)
```

```python
import jax
import jax.numpy as jnp
from jax import lax
from jax.experimental import pallas as pl
from jax.experimental.pallas import tpu as pltpu
from jax.sharding import PartitionSpec as P

MESH = pl.DeviceIdType.MESH
F32 = jnp.float32
BF16 = jnp.bfloat16
I32 = jnp.int32
NEG = -1e30
NX, NZ, NH = 4, 16, 8
HD = 128
G = 8
ROWS = 256
DOC_SLOTS = 48
LEAF_SLOTS = 12
SLOTS = 64
NT = (((1,), (1,)), ((), ()))
Z_ORDER = (8, 7, 9, 6, 10, 5, 11, 4, 12, 3, 13, 2, 14, 1, 15)


def iota(shape, dim):
    return lax.broadcasted_iota(I32, shape, dim)


def dot(a, b):
    return jnp.dot(a, b, preferred_element_type=F32)


def dot_nt(a, b):
    return lax.dot_general(a, b, NT, preferred_element_type=F32)


def onehot(cond):
    return jnp.where(cond, 1.0, 0.0).astype(BF16)


def softmax_parts(scores_of, chunks, chunk, lanes, vt_ref, s_ref, p_ref):
    top = None
    for c in range(chunks):
        s = scores_of(c)
        s_ref[c * chunk:(c + 1) * chunk, :lanes] = s
        peak = jnp.max(s, axis=0, keepdims=True)
        top = peak if top is None else jnp.maximum(top, peak)
    top = top.astype(BF16).astype(F32)
    total = None
    for c in range(chunks):
        p = jnp.exp(s_ref[c * chunk:(c + 1) * chunk, :lanes] - top)
        part = jnp.sum(p, axis=0, keepdims=True)
        total = part if total is None else total + part
        p_ref[c * chunk:(c + 1) * chunk, :lanes] = p.astype(BF16)
    accum = dot(vt_ref[...], p_ref[:chunks * chunk, :lanes])
    return top, total, accum


def kernel(q_ref, len_ref, parent_ref, rl_ref, doc_hbm, leaf_hbm, suf_hbm, w_hbm, out_ref,
           doc, leaf, suf, wv, doc_vt, leaf_vt, suf_vt, wt, qa, oh, ee, s_buf, p_buf, sb, rb, xs, xr, at, ob, db,
           ld, a_zs, a_zr, a_xs, a_xr, b_zs, b_zr, b_xs, b_xr, c_zs, c_zr, c_xs, c_xr, d_s, d_r):
    pos = lax.axis_index("seq")
    head = lax.axis_index("head")
    x, z = pos // NZ, pos % NZ
    quad = z // 4
    scaling = HD ** -0.5

    def at_xz(xx, zz):
        return (xx % NX) * NZ + zz % NZ

    def remote(src, dst, send, recv, seq_id, head_id):
        return pltpu.make_async_remote_copy(
            src_ref=src, dst_ref=dst, send_sem=send, recv_sem=recv,
            device_id=(seq_id, head_id), device_id_type=MESH)

    loads = [pltpu.make_async_copy(h, v, ld.at[i])
             for i, (h, v) in enumerate(((suf_hbm, suf), (doc_hbm, doc), (leaf_hbm, leaf), (w_hbm, wv)))]
    for load in loads:
        load.start()

    barrier = pltpu.get_barrier_semaphore()
    for o in Z_ORDER:
        pl.semaphore_signal(barrier, inc=1, device_id=(at_xz(x, z + o), head), device_id_type=MESH)
    for o in (1, 2, 3):
        pl.semaphore_signal(barrier, inc=1, device_id=(at_xz(x + o, z), head), device_id_type=MESH)
    for o in range(1, NH):
        pl.semaphore_signal(barrier, inc=1, device_id=(pos, (head + o) % NH), device_id_type=MESH)

    qf = q_ref[...].astype(F32)
    qa[pos] = jnp.concatenate([qf[:, g * HD:(g + 1) * HD] for g in range(G)], axis=0).astype(BF16)

    pl.semaphore_wait(barrier, 15 + 3 + 7)

    sends = []
    for o in Z_ORDER:
        c = remote(qa.at[pos], qa.at[pos], a_zs.at[o], a_zr.at[o], at_xz(x, z + o), head)
        c.start()
        sends.append(c)

    eye = onehot(iota((HD, HD), 0) == iota((HD, HD), 1))
    rl = rl_ref[...]
    leaf_hot = onehot(iota((64, ROWS), 0) == rl)
    parents = jnp.broadcast_to(parent_ref[...].astype(F32), (16, 64)).astype(BF16)
    rd = dot(parents, leaf_hot)[:1].astype(I32)
    before = onehot(iota((ROWS, ROWS), 0) < iota((ROWS, ROWS), 1))
    leaf_slot = jnp.sum(leaf_hot.astype(F32) * dot(leaf_hot, before), axis=0, keepdims=True).astype(I32)
    doc_hot = onehot(iota((16, ROWS), 0) == rd)
    doc_slot = jnp.sum(doc_hot.astype(F32) * dot(doc_hot, before), axis=0, keepdims=True).astype(I32)
    row = iota((1, ROWS), 1)

    my_doc = x * 4 + quad
    want = jnp.concatenate([
        jnp.where(rd == my_doc, doc_slot, 128),
        jnp.where(rl == pos, DOC_SLOTS + leaf_slot, 128),
        jnp.full((14, ROWS), 128, I32),
    ], axis=0).astype(F32).astype(BF16)
    for t in range(8):
        lane = iota((ROWS, 256), 1) + t * 256
        spread = onehot(iota((ROWS, 256), 0) == (lane // 32) * 4 + lane % 4)
        wide = dot(want, spread).astype(I32)
        lane = iota((1, 256), 1) + t * 256
        base = ((lane // 4) % 8) * SLOTS
        first = jnp.where(wide[0:1] < 128, wide[0:1] + base, -1)
        second = jnp.where(wide[1:2] < 128, wide[1:2] + base, -1)
        sub = iota((G * SLOTS, 256), 0)
        oh[:, t * 256:(t + 1) * 256] = onehot((sub == first) | (sub == second))

    sub = iota((ROWS, ROWS), 0)
    ee[0] = onehot(sub == jnp.where(rd // 4 == x, (rd % 4) * SLOTS + doc_slot, -1))
    for j in range(4):
        here = (rl // 16 == x) & (rl % 4 == j)
        ee[1 + j] = onehot(sub == jnp.where(here, ((rl // 4) % 4) * SLOTS + DOC_SLOTS + leaf_slot, -1))
        owner = row // 4
        here = (owner // 16 == x) & (owner % 4 == j)
        ee[5 + j] = onehot(sub == jnp.where(here, ((owner // 4) % 4) * SLOTS + 60 + row % 4, -1))

    loads[0].wait()
    for i in range(4):
        suf_vt[:, i * 512:(i + 1) * 512] = dot_nt(eye, suf[1, i]).astype(BF16)
    own_q = jnp.concatenate([qa[pos].astype(F32), jnp.zeros((96, HD), F32)], axis=0).astype(BF16)
    lane4 = iota((1, 128), 1) % 4
    live = jnp.where(lane4 == 0, len_ref[0], jnp.where(lane4 == 1, len_ref[1], jnp.where(
        lane4 == 2, len_ref[2], len_ref[3])))

    def suffix_scores(c):
        s = dot_nt(suf[0, c], own_q) * scaling
        return jnp.where((lane4 == c) & (iota((512, 128), 0) < live), s, NEG)

    top_s, total_s, accum_s = softmax_parts(suffix_scores, 4, 512, 128, suf_vt, s_buf, p_buf)

    def pieces(top, total):
        high = total.astype(BF16).astype(F32)
        return [top, high, total - high]

    packed = jnp.concatenate([accum_s] + pieces(top_s, total_s) + [jnp.zeros((13, 128), F32)], axis=0).astype(BF16)
    lane = iota((128, 512), 1)
    source = iota((128, 512), 0)
    place = onehot((lane % SLOTS >= 60) & (source == (lane // SLOTS) * 4 + lane % 4) & (source < 32))
    placed = dot(packed, place)

    loads[1].wait()
    for c in range(4):
        doc_vt[:, c * 512:(c + 1) * 512] = dot_nt(eye, doc[1, c * 512:(c + 1) * 512, :]).astype(BF16)
    loads[2].wait()
    for c in range(2):
        leaf_vt[:, c * 512:(c + 1) * 512] = dot_nt(eye, leaf[1, c * 512:(c + 1) * 512, :]).astype(BF16)
    loads[3].wait()
    for c in range(2):
        wt[:, c * 512:(c + 1) * 512] = dot_nt(eye, wv[c * 512:(c + 1) * 512, :]).astype(BF16)

    def z_wait(buf, index, send, recv, o):
        remote(buf.at[index], buf.at[index], send.at[o], recv.at[o], pos, head).wait_recv()

    for o in Z_ORDER[::-1]:
        z_wait(qa, at_xz(x, z - o), a_zs, a_zr, o)
    for k in range(4):
        part = qa.at[pl.ds(x * 16 + 4 * k, 4)]
        for o in (1, 2, 3):
            c = remote(part, part, a_xs.at[o * 4 + k], a_xr.at[o * 4 + k], at_xz(x + o, z), head)
            c.start()
            sends.append(c)
    for k in range(4):
        for o in (1, 2, 3):
            part = qa.at[pl.ds(((x - o) % NX) * 16 + 4 * k, 4)]
            remote(part, part, a_xs.at[o * 4 + k], a_xr.at[o * 4 + k], pos, head).wait_recv()

    every_q = qa[...].reshape(64 * 32, HD)
    slot_lane = iota((1, 256), 1) % SLOTS
    for hq in range(2):
        mine = dot(oh[hq * 256:(hq + 1) * 256, :], every_q).astype(BF16)
        top_d, total_d, accum_d = softmax_parts(
            lambda c: dot_nt(doc[0, c * 256:(c + 1) * 256, :], mine) * scaling, 8, 256, 256, doc_vt, s_buf, p_buf)
        top_l, total_l, accum_l = softmax_parts(
            lambda c: dot_nt(leaf[0, c * 256:(c + 1) * 256, :], mine) * scaling, 4, 256, 256, leaf_vt, s_buf, p_buf)
        stats = [
            jnp.where(slot_lane < DOC_SLOTS, d, jnp.where(slot_lane < 60, l, placed[HD + n:HD + n + 1, hq * 256:(hq + 1) * 256]))
            for n, (d, l) in enumerate(zip(pieces(top_d, total_d), pieces(top_l, total_l)))
        ]
        accum = jnp.where(slot_lane < DOC_SLOTS, accum_d, jnp.where(
            slot_lane < 60, accum_l, placed[:HD, hq * 256:(hq + 1) * 256])).astype(BF16)
        gap = jnp.zeros((5, 128), F32)
        stat = jnp.concatenate(
            [v[:, :128] for v in stats] + [gap] + [v[:, 128:] for v in stats] + [gap], axis=0).astype(BF16)
        for c in range(8):
            sb[hq * 8 + c, :, :256] = accum[c * 16:(c + 1) * 16]
            sb[hq * 8 + c, :, 256:] = stat

    for o in Z_ORDER:
        c = remote(sb.at[(z + o) % NZ], rb.at[z], b_zs.at[o], b_zr.at[o], at_xz(x, z + o), head)
        c.start()
        sends.append(c)
    rb[z] = sb[z]
    for o in Z_ORDER[::-1]:
        z_wait(rb, (z - o) % NZ, b_zs, b_zr, o)

    low = iota((16, 128), 1) < 64
    docs, rest = [], None
    for j in range(4):
        got = [rb[4 * k + j].astype(F32) for k in range(4)]
        left = []
        for b, t in ((0, 0), (1, 0), (0, 1), (1, 1), (0, 2), (1, 2)):
            tiles = [v[:, t * 128:(t + 1) * 128] for v in got]
            turned = [pltpu.roll(v, 64, 1) for v in tiles]
            if b == 0:
                halves = [jnp.where(low, tiles[0], turned[1]), jnp.where(low, tiles[2], turned[3])]
            else:
                halves = [jnp.where(low, turned[0], tiles[1]), jnp.where(low, turned[2], tiles[3])]
            left.append(jnp.concatenate(halves, axis=1))
        left = jnp.concatenate(left, axis=0).astype(BF16)
        docs.append(dot(left, ee[0]))
        more = (dot(left, ee[1 + j]), dot(left, ee[5 + j]))
        rest = more if rest is None else (rest[0] + more[0], rest[1] + more[1])

    def merged(parts):
        top = parts[0][1]
        for _, m, _ in parts[1:]:
            top = jnp.maximum(top, m)
        accum, total = None, None
        for a, m, l in parts:
            weight = jnp.exp(m - top)
            accum = a * weight if accum is None else accum + a * weight
            total = l * weight if total is None else total + l * weight
        return accum, top, total

    for a in range(4):
        t, b = a // 2, a % 2
        parts = []
        for got in docs + list(rest):
            s0 = 64 + b * 16 + t * 8
            total = got[s0 + 1:s0 + 2] + got[s0 + 2:s0 + 3]
            parts.append((got[a * 16:(a + 1) * 16], jnp.where(total > 0, got[s0:s0 + 1], NEG), total))
        accum, top, total = merged(parts)
        xs[a] = jnp.concatenate([accum, top, total, jnp.zeros((6, ROWS), F32)], axis=0)

    for o in (2, 1, 3):
        c = remote(xs.at[(x + o) % NX], xr.at[x], b_xs.at[o], b_xr.at[o], at_xz(x + o, z), head)
        c.start()
        sends.append(c)
    xr[x] = xs[x]
    for o in (1, 3, 2):
        z_wait(xr, (x - o) % NX, b_xs, b_xr, o)
    parts = []
    for i in range(NX):
        v = xr[i]
        parts.append((v[:16], v[16:17], v[17:18]))
    accum, _, total = merged(parts)

    def at_index(xx, zz):
        return (zz // 8) * 32 + xx * 8 + zz % 8

    mine = at_index(x, z)
    at[mine] = (accum / total).astype(BF16)
    for o in Z_ORDER:
        c = remote(at.at[mine], at.at[mine], c_zs.at[o], c_zr.at[o], at_xz(x, z + o), head)
        c.start()
        sends.append(c)
    for o in Z_ORDER[::-1]:
        z_wait(at, at_index(x, (z - o) % NZ), c_zs, c_zr, o)
    for k in range(2):
        part = at.at[pl.ds(k * 32 + x * 8, 8)]
        for o in (1, 2, 3):
            c = remote(part, part, c_xs.at[o * 2 + k], c_xr.at[o * 2 + k], at_xz(x + o, z), head)
            c.start()
            sends.append(c)
    for k in range(2):
        for o in (1, 2, 3):
            part = at.at[pl.ds(k * 32 + ((x - o) % NX) * 8, 8)]
            remote(part, part, c_xs.at[o * 2 + k], c_xr.at[o * 2 + k], pos, head).wait_recv()

    share = dot(wt[...], at[...].reshape(1024, ROWS)).T
    for i in range(NH):
        ob[i] = share[i * 32:(i + 1) * 32]
    for o in (4, 3, 5, 2, 6, 1, 7):
        c = remote(ob.at[(head + o) % NH], db.at[head], d_s.at[o], d_r.at[o], pos, (head + o) % NH)
        c.start()
        sends.append(c)
    db[head] = ob[head]
    for o in (1, 7, 2, 6, 3, 5, 4):
        z_wait(db, (head - o) % NH, d_s, d_r, o)
    out = db[0]
    for i in range(1, NH):
        out = out + db[i]
    out_ref[...] = out.astype(BF16)
    for c in sends:
        c.wait_send()


def per_device(queries, doc_kv, leaf_kv, suffix_kv, suffix_len, parent, row_leaf, out_weight):
    vmem = pl.BlockSpec(memory_space=pltpu.VMEM)
    smem = pl.BlockSpec(memory_space=pltpu.SMEM)
    hbm = pl.BlockSpec(memory_space=pl.ANY)
    dma = pltpu.SemaphoreType.DMA
    return pl.pallas_call(
        kernel,
        out_shape=jax.ShapeDtypeStruct((32, 128), BF16),
        in_specs=[vmem, smem, vmem, vmem, hbm, hbm, hbm, hbm],
        out_specs=vmem,
        scratch_shapes=[
            pltpu.VMEM((2, 2048, HD), BF16),
            pltpu.VMEM((2, 1024, HD), BF16),
            pltpu.VMEM((2, 4, 512, HD), BF16),
            pltpu.VMEM((1024, 128), BF16),
            pltpu.VMEM((HD, 2048), BF16),
            pltpu.VMEM((HD, 1024), BF16),
            pltpu.VMEM((HD, 2048), BF16),
            pltpu.VMEM((128, 1024), BF16),
            pltpu.VMEM((64, 32, HD), BF16),
            pltpu.VMEM((512, 2048), BF16),
            pltpu.VMEM((9, ROWS, ROWS), BF16),
            pltpu.VMEM((2048, 256), F32),
            pltpu.VMEM((2048, 256), BF16),
            pltpu.VMEM((16, 16, 384), BF16),
            pltpu.VMEM((16, 16, 384), BF16),
            pltpu.VMEM((4, 24, ROWS), F32),
            pltpu.VMEM((4, 24, ROWS), F32),
            pltpu.VMEM((64, 16, ROWS), BF16),
            pltpu.VMEM((8, 32, 128), F32),
            pltpu.VMEM((8, 32, 128), F32),
            dma((4,)),
            dma((16,)), dma((16,)), dma((16,)), dma((16,)),
            dma((16,)), dma((16,)), dma((4,)), dma((4,)),
            dma((16,)), dma((16,)), dma((8,)), dma((8,)),
            dma((8,)), dma((8,)),
        ],
        compiler_params=pltpu.CompilerParams(
            collective_id=0, has_side_effects=True, vmem_limit_bytes=48 << 20),
        name="tree_attention",
    )(queries, suffix_len, parent.reshape(1, -1), row_leaf.reshape(1, -1), doc_kv, leaf_kv, suffix_kv, out_weight)


def solution(mesh):
    in_specs = (
        P("seq", "head"),
        P(None, "seq", "head"),
        P(None, "seq", "head"),
        P(None, "seq", None, "head"),
        P("seq"),
        P(),
        P(),
        P("head", "seq"),
    )
    return jax.shard_map(
        per_device, mesh=mesh, in_specs=in_specs, out_specs=P("head", "seq"), check_vma=False)
```

```python
import jax
import jax.numpy as jnp
from jax import lax
from jax.experimental import pallas as pl
from jax.experimental.pallas import tpu as pltpu
from jax.sharding import PartitionSpec as P

MESH = pl.DeviceIdType.MESH
F32 = jnp.float32
BF16 = jnp.bfloat16
I32 = jnp.int32
NEG = -1e30
NX, NZ, NH = 4, 16, 8
HD = 128
G = 8
ROWS = 256
DOC_SLOTS = 48
LEAF_SLOTS = 12
RATE = HD ** -0.5 * 1.4426950408889634
SLOTS = 64
NT = (((1,), (1,)), ((), ()))
Z_FAR = (8, 7, 9, 6, 10, 5, 11, 4, 12, 3, 13, 2, 14, 1, 15)
Z_NEAR = Z_FAR[::-1]
Z_STEP = (4, 12, 3, 13, 2, 14, 1, 15)


def iota(shape, dim):
    return lax.broadcasted_iota(I32, shape, dim)


def dot(a, b):
    return jnp.dot(a, b, preferred_element_type=F32)


def dot_nt(a, b):
    return lax.dot_general(a, b, NT, preferred_element_type=F32)


def onehot(cond):
    return jnp.where(cond, 1.0, 0.0).astype(BF16)


def softmax_parts(scores_of, chunks, chunk, lanes, vt_ref, s_ref, p_ref):
    top = None
    for c in range(chunks):
        s = scores_of(c)
        s_ref[c * chunk:(c + 1) * chunk, :lanes] = s
        peak = jnp.max(s, axis=0, keepdims=True)
        top = peak if top is None else jnp.maximum(top, peak)
    top = top.astype(BF16).astype(F32)
    total = None
    for c in range(chunks):
        p = jnp.exp2(s_ref[c * chunk:(c + 1) * chunk, :lanes] * RATE - top * RATE)
        part = jnp.sum(p, axis=0, keepdims=True)
        total = part if total is None else total + part
        p_ref[c * chunk:(c + 1) * chunk, :lanes] = p.astype(BF16)
    accum = dot(vt_ref[...], p_ref[:chunks * chunk, :lanes])
    return top, total, accum


def kernel(q_hbm, len_ref, parent_hbm, rl_hbm, doc_hbm, leaf_hbm, suf_hbm, w_hbm, out_ref,
           q_ref, parent_ref, rl_ref, doc, leaf, suf, wv, doc_vt, leaf_vt, suf_vt, wx, qa, oh, ee, s_buf, p_buf, sb, rb, xs, xr, at, ob, db,
           ld, a_zs, a_zr, a_xs, a_xr, b_zs, b_zr, b_xs, b_xr, c_zs, c_zr, w_s, w_r, d_s, d_r):
    pos = lax.axis_index("seq")
    head = lax.axis_index("head")
    x, z = pos // NZ, pos % NZ
    quad = z // 4

    def at_xz(xx, zz):
        return (xx % NX) * NZ + zz % NZ

    def remote(src, dst, send, recv, seq_id, head_id):
        return pltpu.make_async_remote_copy(
            src_ref=src, dst_ref=dst, send_sem=send, recv_sem=recv,
            device_id=(seq_id, head_id), device_id_type=MESH)

    loads = [pltpu.make_async_copy(h, v, ld.at[i])
             for i, (h, v) in enumerate((
                 (suf_hbm, suf), (doc_hbm, doc), (leaf_hbm, leaf), (w_hbm, wv), (q_hbm, q_ref),
                 (parent_hbm, parent_ref), (rl_hbm, rl_ref)))]
    for i in (4, 5, 6, 0, 1, 2, 3):
        loads[i].start()

    barrier = pltpu.get_barrier_semaphore()
    for o in Z_STEP:
        pl.semaphore_signal(barrier, inc=1, device_id=(at_xz(x, z + o), head), device_id_type=MESH)
    for i in range(NX):
        for o in range(NH):
            if i or o:
                pl.semaphore_signal(
                    barrier, inc=1, device_id=(at_xz(x + i, z), (head + o) % NH), device_id_type=MESH)

    loads[4].wait()
    qf = q_ref[...].astype(F32)
    qa[pos] = jnp.concatenate([qf[:, g * HD:(g + 1) * HD] for g in range(G)], axis=0).astype(BF16)

    eye = onehot(iota((HD, HD), 0) == iota((HD, HD), 1))
    loads[5].wait()
    loads[6].wait()
    rl = rl_ref[...]
    leaf_hot = onehot(iota((64, ROWS), 0) == rl)
    parents = jnp.broadcast_to(parent_ref[...].astype(F32), (16, 64)).astype(BF16)
    rd = dot(parents, leaf_hot)[:1].astype(I32)
    before = onehot(iota((ROWS, ROWS), 0) < iota((ROWS, ROWS), 1))
    leaf_slot = jnp.sum(leaf_hot.astype(F32) * dot(leaf_hot, before), axis=0, keepdims=True).astype(I32)
    doc_hot = onehot(iota((16, ROWS), 0) == rd)
    doc_slot = jnp.sum(doc_hot.astype(F32) * dot(doc_hot, before), axis=0, keepdims=True).astype(I32)
    row = iota((1, ROWS), 1)

    my_doc = x * 4 + quad
    want = jnp.concatenate([
        jnp.where(rd == my_doc, doc_slot, 128),
        jnp.where(rl == pos, DOC_SLOTS + leaf_slot, 128),
        jnp.full((14, ROWS), 128, I32),
    ], axis=0).astype(F32).astype(BF16)
    for t in range(8):
        lane = iota((ROWS, 256), 1) + t * 256
        spread = onehot(iota((ROWS, 256), 0) == (lane // 32) * 4 + lane % 4)
        wide = dot(want, spread).astype(I32)
        lane = iota((1, 256), 1) + t * 256
        base = ((lane // 4) % 8) * SLOTS
        first = jnp.where(wide[0:1] < 128, wide[0:1] + base, -1)
        second = jnp.where(wide[1:2] < 128, wide[1:2] + base, -1)
        sub = iota((G * SLOTS, 256), 0)
        oh[:, t * 256:(t + 1) * 256] = onehot((sub == first) | (sub == second))

    pl.semaphore_wait(barrier, len(Z_STEP) + NX * NH - 1)

    sends = []

    def push(src, dst, send, recv, seq_id, head_id):
        c = remote(src, dst, send, recv, seq_id, head_id)
        c.start()
        sends.append(c)

    for o in Z_STEP:
        push(qa.at[pos], qa.at[pos], a_zs.at[16 - o], a_zr.at[16 - o], at_xz(x, z + o), head)
    for r in (0, 1, 15, 2, 14, 3, 13, 4, 12, 5, 11, 6, 10, 7, 9, 8):
        block = qa.at[at_xz(x, z + r)]
        if r:
            remote(block, block, a_zs.at[r], a_zr.at[r], pos, head).wait_recv()
        if 1 <= r <= 4:
            push(block, block, a_zs.at[r + 4], a_zr.at[r + 4], at_xz(x, z - 4), head)
        if 13 <= r <= 15:
            push(block, block, a_zs.at[r - 4], a_zr.at[r - 4], at_xz(x, z + 4), head)
        for i in (2, 1, 3):
            push(block, block, a_xs.at[i * 16 + r], a_xr.at[i * 16 + r], at_xz(x + i, z), head)

    loads[0].wait()
    for i in range(4):
        suf_vt[:, i * 512:(i + 1) * 512] = dot_nt(eye, suf[1, i]).astype(BF16)
    own_q = jnp.concatenate([qa[pos].astype(F32), jnp.zeros((96, HD), F32)], axis=0).astype(BF16)
    lane4 = iota((1, 128), 1) % 4
    live = jnp.where(lane4 == 0, len_ref[0], jnp.where(lane4 == 1, len_ref[1], jnp.where(
        lane4 == 2, len_ref[2], len_ref[3])))

    def suffix_scores(c):
        s = dot_nt(suf[0, c], own_q)
        return jnp.where((lane4 == c) & (iota((512, 128), 0) < live), s, NEG)

    top_s, total_s, accum_s = softmax_parts(suffix_scores, 4, 512, 128, suf_vt, s_buf, p_buf)

    def pieces(top, total):
        high = total.astype(BF16).astype(F32)
        return [top, high, total - high]

    packed = jnp.concatenate([accum_s] + pieces(top_s, total_s) + [jnp.zeros((13, 128), F32)], axis=0).astype(BF16)
    lane = iota((128, 512), 1)
    source = iota((128, 512), 0)
    place = onehot((lane % SLOTS >= 60) & (source == (lane // SLOTS) * 4 + lane % 4) & (source < 32))
    placed = dot(packed, place)

    loads[1].wait()
    for c in range(4):
        doc_vt[:, c * 512:(c + 1) * 512] = dot_nt(eye, doc[1, c * 512:(c + 1) * 512, :]).astype(BF16)
    loads[2].wait()
    for c in range(2):
        leaf_vt[:, c * 512:(c + 1) * 512] = dot_nt(eye, leaf[1, c * 512:(c + 1) * 512, :]).astype(BF16)
    for r in range(16):
        for i in (1, 3, 2):
            block = qa.at[at_xz(x - i, z + r)]
            remote(block, block, a_xs.at[i * 16 + r], a_xr.at[i * 16 + r], pos, head).wait_recv()

    every_q = qa[...].reshape(64 * 32, HD)
    slot_lane = iota((1, 256), 1) % SLOTS
    for hq in range(2):
        mine = dot(oh[hq * 256:(hq + 1) * 256, :], every_q).astype(BF16)
        top_d, total_d, accum_d = softmax_parts(
            lambda c: dot_nt(doc[0, c * 256:(c + 1) * 256, :], mine), 8, 256, 256, doc_vt, s_buf, p_buf)
        top_l, total_l, accum_l = softmax_parts(
            lambda c: dot_nt(leaf[0, c * 256:(c + 1) * 256, :], mine), 4, 256, 256, leaf_vt, s_buf, p_buf)
        stats = [
            jnp.where(slot_lane < DOC_SLOTS, d, jnp.where(slot_lane < 60, l, placed[HD + n:HD + n + 1, hq * 256:(hq + 1) * 256]))
            for n, (d, l) in enumerate(zip(pieces(top_d, total_d), pieces(top_l, total_l)))
        ]
        accum = jnp.where(slot_lane < DOC_SLOTS, accum_d, jnp.where(
            slot_lane < 60, accum_l, placed[:HD, hq * 256:(hq + 1) * 256])).astype(BF16)
        gap = jnp.zeros((5, 128), F32)
        stat = jnp.concatenate(
            [v[:, :128] for v in stats] + [gap] + [v[:, 128:] for v in stats] + [gap], axis=0).astype(BF16)
        for c in range(8):
            sb[hq * 8 + c, :, :256] = accum[c * 16:(c + 1) * 16]
            sb[hq * 8 + c, :, 256:] = stat
        for c in range(8):
            to = hq * 8 + (z + 4 + c) % 8

            @pl.when(to != z)
            def _():
                remote(sb.at[to], rb.at[z], b_zs.at[to], b_zr.at[z], at_xz(x, to), head).start()

    loads[3].wait()
    for o in (2, 1, 3):
        push(wv.at[:, (x + o) % NX], wx.at[x], w_s.at[o], w_r.at[o], at_xz(x + o, z), head)
    wx[x] = wv[:, x]

    sub = iota((ROWS, ROWS), 0)
    ee[0] = onehot(sub == jnp.where(rd // 4 == x, (rd % 4) * SLOTS + doc_slot, -1))
    for j in range(4):
        here = (rl // 16 == x) & (rl % 4 == j)
        ee[1 + j] = onehot(sub == jnp.where(here, ((rl // 4) % 4) * SLOTS + DOC_SLOTS + leaf_slot, -1))
        owner = row // 4
        here = (owner // 16 == x) & (owner % 4 == j)
        ee[5 + j] = onehot(sub == jnp.where(here, ((owner // 4) % 4) * SLOTS + 60 + row % 4, -1))

    rb[z] = sb[z]
    for o in Z_NEAR:
        i = (z - o) % NZ
        c = remote(sb.at[i], rb.at[i], b_zs.at[i], b_zr.at[i], pos, head)
        c.wait_send()
        c.wait_recv()

    low = iota((16, 128), 1) < 64
    docs, rest = [], None
    for j in range(4):
        got = [rb[4 * k + j].astype(F32) for k in range(4)]
        left = []
        for b, t in ((0, 0), (1, 0), (0, 1), (1, 1), (0, 2), (1, 2)):
            tiles = [v[:, t * 128:(t + 1) * 128] for v in got]
            turned = [pltpu.roll(v, 64, 1) for v in tiles]
            if b == 0:
                halves = [jnp.where(low, tiles[0], turned[1]), jnp.where(low, tiles[2], turned[3])]
            else:
                halves = [jnp.where(low, turned[0], tiles[1]), jnp.where(low, turned[2], tiles[3])]
            left.append(jnp.concatenate(halves, axis=1))
        left = jnp.concatenate(left, axis=0).astype(BF16)
        docs.append(dot(left, ee[0]))
        more = (dot(left, ee[1 + j]), dot(left, ee[5 + j]))
        rest = more if rest is None else (rest[0] + more[0], rest[1] + more[1])

    def merged(parts):
        top = parts[0][1]
        for _, m, _ in parts[1:]:
            top = jnp.maximum(top, m)
        accum, total = None, None
        for a, m, l in parts:
            weight = jnp.exp2((m - top) * RATE)
            accum = a * weight if accum is None else accum + a * weight
            total = l * weight if total is None else total + l * weight
        return accum, top, total

    for a in range(4):
        t, b = a // 2, a % 2
        parts = []
        for got in docs + list(rest):
            s0 = 64 + b * 16 + t * 8
            total = got[s0 + 1:s0 + 2] + got[s0 + 2:s0 + 3]
            parts.append((got[a * 16:(a + 1) * 16], jnp.where(total > 0, got[s0:s0 + 1], NEG), total))
        accum, top, total = merged(parts)
        xs[a] = jnp.concatenate([accum, top, total, jnp.zeros((6, ROWS), F32)], axis=0)

    for o in (2, 1, 3):
        push(xs.at[(x + o) % NX], xr.at[x], b_xs.at[o], b_xr.at[o], at_xz(x + o, z), head)
    xr[x] = xs[x]
    for o in (1, 3, 2):
        block = xr.at[(x - o) % NX]
        remote(block, block, b_xs.at[o], b_xr.at[o], pos, head).wait_recv()
    parts = []
    for i in range(NX):
        v = xr[i]
        parts.append((v[:16], v[16:17], v[17:18]))
    accum, _, total = merged(parts)

    at[z] = (accum / total).astype(BF16)
    for o in Z_FAR:
        push(at.at[z], at.at[z], c_zs.at[16 - o], c_zr.at[16 - o], at_xz(x, z + o), head)
    for o in (1, 3, 2):
        block = wx.at[(x - o) % NX]
        remote(block, block, w_s.at[o], w_r.at[o], pos, head).wait_recv()
    for r in Z_NEAR:
        block = at.at[(z + r) % NZ]
        remote(block, block, c_zs.at[r], c_zr.at[r], pos, head).wait_recv()

    eye = onehot(iota((ROWS, ROWS), 0) == iota((ROWS, ROWS), 1))
    attention = dot_nt(eye, at[...].reshape(ROWS, ROWS)).astype(BF16)
    for i in (2, 1, 3, 0):
        to = (x + i) % NX
        share = dot(attention, wx[to].reshape(2 * HD, HD)).astype(BF16)
        for n in range(NH):
            ob[to, n] = share[n * 32:(n + 1) * 32]
        for o in (4, 3, 5, 2, 6, 1, 7, 0):
            if i or o:
                n = (head + o) % NH
                push(ob.at[to, n], db.at[x, head], d_s.at[i * 8 + o], d_r.at[i * 8 + o], at_xz(to, z), n)
    db[x, head] = ob[x, head]
    for i in (1, 3, 2, 0):
        for o in range(NH):
            if i or o:
                block = db.at[(x - i) % NX, (head - o) % NH]
                remote(block, block, d_s.at[i * 8 + o], d_r.at[i * 8 + o], pos, head).wait_recv()
    out_ref[...] = jnp.sum(db[...].reshape(NX * NH, 32, HD).astype(F32), axis=0).astype(BF16)
    for c in sends:
        c.wait_send()


def per_device(queries, doc_kv, leaf_kv, suffix_kv, suffix_len, parent, row_leaf, out_weight):
    vmem = pl.BlockSpec(memory_space=pltpu.VMEM)
    smem = pl.BlockSpec(memory_space=pltpu.SMEM)
    hbm = pl.BlockSpec(memory_space=pl.ANY)
    dma = pltpu.SemaphoreType.DMA
    return pl.pallas_call(
        kernel,
        out_shape=jax.ShapeDtypeStruct((32, 128), BF16),
        in_specs=[hbm, smem, hbm, hbm, hbm, hbm, hbm, hbm],
        out_specs=vmem,
        scratch_shapes=[
            pltpu.VMEM((4, 1024), BF16),
            pltpu.VMEM((1, 64), I32),
            pltpu.VMEM((1, 256), I32),
            pltpu.VMEM((2, 2048, HD), BF16),
            pltpu.VMEM((2, 1024, HD), BF16),
            pltpu.VMEM((2, 4, 512, HD), BF16),
            pltpu.VMEM((2, NX, HD, HD), BF16),
            pltpu.VMEM((HD, 2048), BF16),
            pltpu.VMEM((HD, 1024), BF16),
            pltpu.VMEM((HD, 2048), BF16),
            pltpu.VMEM((NX, 2, HD, HD), BF16),
            pltpu.VMEM((64, 32, HD), BF16),
            pltpu.VMEM((512, 2048), BF16),
            pltpu.VMEM((9, ROWS, ROWS), BF16),
            pltpu.VMEM((2048, 256), F32),
            pltpu.VMEM((2048, 256), BF16),
            pltpu.VMEM((16, 16, 384), BF16),
            pltpu.VMEM((16, 16, 384), BF16),
            pltpu.VMEM((4, 24, ROWS), F32),
            pltpu.VMEM((4, 24, ROWS), F32),
            pltpu.VMEM((16, 16, ROWS), BF16),
            pltpu.VMEM((NX, NH, 32, HD), BF16),
            pltpu.VMEM((NX, NH, 32, HD), BF16),
            dma((7,)),
            dma((16,)), dma((16,)), dma((64,)), dma((64,)),
            dma((16,)), dma((16,)), dma((4,)), dma((4,)),
            dma((16,)), dma((16,)), dma((4,)), dma((4,)),
            dma((32,)), dma((32,)),
        ],
        compiler_params=pltpu.CompilerParams(
            collective_id=0, has_side_effects=True, vmem_limit_bytes=62 << 20),
        name="tree_attention",
    )(queries, suffix_len, parent.reshape(1, -1), row_leaf.reshape(1, -1), doc_kv, leaf_kv, suffix_kv,
      out_weight.reshape(2, NX, HD, HD))


def solution(mesh):
    in_specs = (
        P("seq", "head"),
        P(None, "seq", "head"),
        P(None, "seq", "head"),
        P(None, "seq", None, "head"),
        P("seq"),
        P(),
        P(),
        P("head", "seq"),
    )
    return jax.shard_map(
        per_device, mesh=mesh, in_specs=in_specs, out_specs=P("head", "seq"), check_vma=False)
```

```python
import jax
import jax.numpy as jnp
from jax import lax
from jax.experimental import pallas as pl
from jax.experimental.pallas import tpu as pltpu
from jax.sharding import PartitionSpec as P

MESH = pl.DeviceIdType.MESH
F32 = jnp.float32
BF16 = jnp.bfloat16
I32 = jnp.int32
NEG = -2.0 ** 100
NX, NZ, NH = 4, 16, 8
HD = 128
G = 8
ROWS = 256
DOC_SLOTS = 48
LEAF_SLOTS = 12
RATE = HD ** -0.5 * 1.4426950408889634
LEAF_AT = G // 2 * DOC_SLOTS
NT = (((1,), (1,)), ((), ()))
Z_FAR = (8, 7, 9, 6, 10, 5, 11, 4, 12, 3, 13, 2, 14, 1, 15)
Z_NEAR = Z_FAR[::-1]
Z_STEP = (4, 12, 3, 13, 2, 14, 1, 15)


def iota(shape, dim):
    return lax.broadcasted_iota(I32, shape, dim)


def dot(a, b):
    return jnp.dot(a, b, preferred_element_type=F32)


def dot_nt(a, b):
    return lax.dot_general(a, b, NT, preferred_element_type=F32)


def onehot(cond):
    return jnp.where(cond, 1.0, 0.0).astype(BF16)


def merged(parts):
    top = parts[0][1]
    for _, m, _ in parts[1:]:
        top = jnp.maximum(top, m)
    accum, total = None, None
    for a, m, l in parts:
        weight = jnp.exp2((m - top) * RATE)
        accum = a * weight if accum is None else accum + a * weight
        total = l * weight if total is None else total + l * weight
    return accum, top, total


def attend(scores_of, chunks, chunk, vt_ref):
    parts = []
    for c in range(chunks):
        s = scores_of(c)
        top = jnp.max(s, axis=0, keepdims=True)
        p = jnp.exp2(s * RATE - top * RATE)
        accum = dot(vt_ref[:, c * chunk:(c + 1) * chunk], p.astype(BF16))
        parts.append((accum, top, jnp.sum(p, axis=0, keepdims=True)))
    accum, top, total = merged(parts)
    level = top + jnp.log2(total) * (1 / RATE)
    high = level.astype(BF16).astype(F32)
    return accum / total, high, level - high


def turn(v, lanes):
    return pltpu.roll(v, lanes % 128, 1) if lanes % 128 else v


def kernel(q_hbm, len_ref, parent_hbm, rl_hbm, doc_hbm, leaf_hbm, suf_hbm, w_hbm, out_ref,
           q_ref, parent_ref, rl_ref, doc, leaf, suf, wv, doc_vt, leaf_vt, suf_vt, wx, qa, oh, ed, el, es, sl, rl_in, sb, rb, xs, xr, at, ob, db,
           ld, a_zs, a_zr, a_xs, a_xr, l_zs, l_zr, b_zs, b_zr, b_xs, b_xr, c_zs, c_zr, w_s, w_r, d_s, d_r):
    pos = lax.axis_index("seq")
    head = lax.axis_index("head")
    x, z = pos // NZ, pos % NZ
    quad = z // 4

    def at_xz(xx, zz):
        return (xx % NX) * NZ + zz % NZ

    def remote(src, dst, send, recv, seq_id, head_id):
        return pltpu.make_async_remote_copy(
            src_ref=src, dst_ref=dst, send_sem=send, recv_sem=recv,
            device_id=(seq_id, head_id), device_id_type=MESH)

    loads = [pltpu.make_async_copy(h, v, ld.at[i])
             for i, (h, v) in enumerate((
                 (suf_hbm, suf), (doc_hbm, doc), (leaf_hbm, leaf), (w_hbm, wv), (q_hbm, q_ref),
                 (parent_hbm, parent_ref), (rl_hbm, rl_ref)))]
    for i in (4, 5, 6, 0, 1, 2, 3):
        loads[i].start()

    barrier = pltpu.get_barrier_semaphore()
    for o in Z_STEP:
        pl.semaphore_signal(barrier, inc=1, device_id=(at_xz(x, z + o), head), device_id_type=MESH)
    for i in range(NX):
        for o in range(NH):
            if i or o:
                pl.semaphore_signal(
                    barrier, inc=1, device_id=(at_xz(x + i, z), (head + o) % NH), device_id_type=MESH)

    loads[4].wait()
    qf = q_ref[...].astype(F32)
    qa[pos] = jnp.concatenate([qf[:, g * HD:(g + 1) * HD] for g in range(G)], axis=0).astype(BF16)

    eye = onehot(iota((HD, HD), 0) == iota((HD, HD), 1))
    loads[5].wait()
    loads[6].wait()
    rl = rl_ref[...]
    leaf_hot = onehot(iota((64, ROWS), 0) == rl)
    parents = jnp.broadcast_to(parent_ref[...].astype(F32), (16, 64)).astype(BF16)
    rd = dot(parents, leaf_hot)[:1].astype(I32)
    before = onehot(iota((ROWS, ROWS), 0) < iota((ROWS, ROWS), 1))
    leaf_slot = jnp.sum(leaf_hot.astype(F32) * dot(leaf_hot, before), axis=0, keepdims=True).astype(I32)
    doc_hot = onehot(iota((16, ROWS), 0) == rd)
    doc_slot = jnp.sum(doc_hot.astype(F32) * dot(doc_hot, before), axis=0, keepdims=True).astype(I32)
    row = iota((1, ROWS), 1)

    my_doc = x * 4 + quad
    want = jnp.concatenate([
        jnp.where(rd == my_doc, doc_slot, 128),
        jnp.where(rl == pos, leaf_slot, 128),
        jnp.full((14, ROWS), 128, I32),
    ], axis=0).astype(F32).astype(BF16)
    for t in range(NX):
        lane = iota((ROWS, 256), 1)
        spread = onehot(iota((ROWS, 256), 0) == t * 64 + (lane // 16) * 4 + lane % 4)
        wide = dot(want, spread).astype(I32)
        a = (iota((1, 256), 1) // 4) % 4
        first = jnp.where(wide[0:1] < 128, wide[0:1] + a * DOC_SLOTS, -1)
        second = jnp.where(wide[1:2] < 128, wide[1:2] + (LEAF_AT + a * LEAF_SLOTS), -1)
        sub = iota((256, 256), 0)
        oh[t] = onehot((sub == first) | (sub == second))

    pl.semaphore_wait(barrier, len(Z_STEP) + NX * NH - 1)

    sends = []

    def push(src, dst, send, recv, seq_id, head_id):
        c = remote(src, dst, send, recv, seq_id, head_id)
        c.start()
        sends.append(c)

    for o in Z_STEP:
        push(qa.at[pos], qa.at[pos], a_zs.at[16 - o], a_zr.at[16 - o], at_xz(x, z + o), head)
    for r in (0, 1, 15, 2, 14, 3, 13, 4, 12, 5, 11, 6, 10, 7, 9, 8):
        block = qa.at[at_xz(x, z + r)]
        if r:
            remote(block, block, a_zs.at[r], a_zr.at[r], pos, head).wait_recv()
        if 1 <= r <= 4:
            push(block, block, a_zs.at[r + 4], a_zr.at[r + 4], at_xz(x, z - 4), head)
        if 13 <= r <= 15:
            push(block, block, a_zs.at[r - 4], a_zr.at[r - 4], at_xz(x, z + 4), head)
        for i in (2, 1, 3):
            push(block, block, a_xs.at[i * 16 + r], a_xr.at[i * 16 + r], at_xz(x + i, z), head)

    loads[0].wait()
    for i in range(4):
        suf_vt[:, i * 512:(i + 1) * 512] = dot_nt(eye, suf[1, i]).astype(BF16)
    own_q = jnp.concatenate([qa[pos].astype(F32), jnp.zeros((96, HD), F32)], axis=0).astype(BF16)
    lane4 = iota((1, 128), 1) % 4
    live = jnp.where(lane4 == 0, len_ref[0], jnp.where(lane4 == 1, len_ref[1], jnp.where(
        lane4 == 2, len_ref[2], len_ref[3])))

    def suffix_scores(c):
        s = dot_nt(suf[0, c], own_q)
        return jnp.where((lane4 == c) & (iota((512, 128), 0) < live), s, NEG)

    accum, high, low = attend(suffix_scores, 4, 512, suf_vt)

    def send_parts(out, into, send, recv, pair):
        def start(c):
            to = pair * 4 + (z + c) % 4
            remote(out.at[to], into.at[z], send.at[to], recv.at[z], at_xz(x, to), head).start()

        @pl.when(z // 4 == pair)
        def _():
            for c in (1, 2, 3):
                start(c)

        @pl.when(z // 4 != pair)
        def _():
            for c in range(4):
                start(c)

    lane = iota((1, 128), 1)
    stat = jnp.concatenate([high, low, jnp.zeros((14, 128), F32)], axis=0)
    for pair in range(4):
        a0, a1, v = turn(accum, -8 * pair), turn(accum, 8 - 8 * pair), turn(stat, 16 - 8 * pair)
        for c in range(4):
            sl[pair * 4 + c] = jnp.where(lane < 8, a0[c * 32:c * 32 + 16], jnp.where(
                lane < 16, a1[c * 32 + 16:c * 32 + 32], v)).astype(BF16)
        send_parts(sl, rl_in, l_zs, l_zr, pair)

    loads[1].wait()
    for c in range(4):
        doc_vt[:, c * 512:(c + 1) * 512] = dot_nt(eye, doc[1, c * 512:(c + 1) * 512, :]).astype(BF16)
    loads[2].wait()
    for c in range(2):
        leaf_vt[:, c * 512:(c + 1) * 512] = dot_nt(eye, leaf[1, c * 512:(c + 1) * 512, :]).astype(BF16)
    halves = [None, None]
    for i in (0, 1, 3, 2):
        plane = (x - i) % NX
        if i:
            for r in range(16):
                block = qa.at[at_xz(plane, z + r)]
                remote(block, block, a_xs.at[i * 16 + r], a_xr.at[i * 16 + r], pos, head).wait_recv()
        got = qa[pl.ds(plane * NZ, NZ)]
        for hq in range(2):
            more = dot(oh[plane], got[:, hq * 16:(hq + 1) * 16].reshape(256, HD))
            halves[hq] = more if halves[hq] is None else halves[hq] + more
    halves = [v.astype(BF16) for v in halves]
    rest = jnp.zeros((32, HD), BF16)

    mine = jnp.concatenate([halves[0][LEAF_AT:LEAF_AT + 48], halves[1][LEAF_AT:LEAF_AT + 48], rest], axis=0)
    accum, high, low = attend(lambda c: dot_nt(leaf[0, c * 512:(c + 1) * 512, :], mine), 2, 512, leaf_vt)
    packed = jnp.concatenate([accum, high, low, jnp.zeros((14, 128), F32)], axis=0).astype(BF16)
    source = iota((128, 512), 0)
    place = iota((128, 512), 1)
    leaf_part = dot(packed, onehot(
        (place % 128 >= 96) & (place % 128 < 120) & (source == (place // 128) * 24 + place % 128 - 96)))

    spread = iota((16, 128), 0) == iota((16, 128), 1) // 8
    spread = spread & (iota((16, 128), 1) < 120)
    gather = onehot((iota((128, 128), 1) >= 120) & (iota((128, 128), 0) % 8 == iota((128, 128), 1) - 120))
    for pair in range(4):
        mine = jnp.concatenate([halves[pair // 2][(pair % 2) * 96:(pair % 2) * 96 + 96], rest], axis=0)
        accum, high, low = attend(lambda c: dot_nt(doc[0, c * 512:(c + 1) * 512, :], mine), 4, 512, doc_vt)
        other = leaf_part[:, pair * 128:(pair + 1) * 128]
        accum = jnp.where(lane < 96, accum, other[:HD])
        high = jnp.where(lane < 96, high, other[HD:HD + 1])
        low = jnp.where(lane < 96, low, other[HD + 1:HD + 2])
        both = jnp.concatenate([jnp.where(spread, high, 0.0), jnp.where(spread, low, 0.0)], axis=0).astype(BF16)
        both = dot(both, gather)
        for c in range(4):
            sb[pair * 4 + c] = jnp.where(lane < 120, accum[c * 32:(c + 1) * 32], both).astype(BF16)
        send_parts(sb, rb, b_zs, b_zr, pair)

    loads[3].wait()
    for o in (2, 1, 3):
        to = (x + o) % NX
        push(wv.at[:, to // 2, :, to % 2], wx.at[x], w_s.at[o], w_r.at[o], at_xz(x + o, z), head)
    wx[x] = wv[:, x // 2, :, x % 2]

    sub = iota((512, ROWS), 0)
    for b in range(2):
        cols = slice(b * ROWS, (b + 1) * ROWS)
        ed[:, cols] = onehot(sub == jnp.where(rd // 4 == x, (rd % 4) * 128 + b * DOC_SLOTS + doc_slot, -1))
        el[:, cols] = onehot(sub == jnp.where(
            rl // 16 == x, (rl % 4) * 128 + (rl // 4) % 4 * 32 + b * LEAF_SLOTS + leaf_slot, -1))
        es[:, cols] = onehot(sub[:128] == jnp.where(row // 64 == x, (row // 4) % 16 * 8 + b * 4 + row % 4, -1))

    def take(out, into, send, recv):
        into[z] = out[z]
        for o in Z_NEAR:
            i = (z - o) % NZ
            c = remote(out.at[i], into.at[i], send.at[i], recv.at[i], pos, head)
            c.wait_send()
            c.wait_recv()

    take(sl, rl_in, l_zs, l_zr)
    got = [rl_in[i].astype(F32) for i in range(16)]

    def collect(first, rows):
        v = jnp.zeros((rows, 128), F32)
        for i in range(16):
            v = jnp.where(lane // 8 == i, turn(got[i][:rows], 8 * i - first), v)
        return v

    left = jnp.concatenate([collect(0, 16), collect(8, 16), collect(16, 8)], axis=0).astype(BF16)
    from_suffix = dot(left, es[...])

    take(sb, rb, b_zs, b_zr)
    scatter = onehot((iota((128, 128), 0) >= 120) & (iota((128, 128), 0) - 120 == iota((128, 128), 1) % 8))
    stats = dot(rb[...].reshape(512, 128), scatter)
    gap = jnp.zeros((6, 128), F32)
    got = []
    for i in range(16):
        high = jnp.sum(jnp.where(spread, stats[i * 32:i * 32 + 16], 0.0), axis=0, keepdims=True)
        low = jnp.sum(jnp.where(spread, stats[i * 32 + 16:i * 32 + 32], 0.0), axis=0, keepdims=True)
        got.append(jnp.concatenate([rb[i].astype(F32), high, low, gap], axis=0))
    left, leaves = [], []
    for j in range(4):
        left.append(jnp.concatenate([got[4 * k + j] for k in range(4)], axis=1))
        v = turn(got[j], 32)
        for k in range(1, 4):
            v = jnp.where(lane // 32 == k, turn(got[4 * k + j], 32 + 32 * k), v)
        leaves.append(v)
    from_leaf = dot(jnp.concatenate(leaves, axis=1).astype(BF16), el[...])
    from_doc = dot(jnp.concatenate(left, axis=0).astype(BF16), ed[...])

    for b in range(2):
        cols = slice(b * ROWS, (b + 1) * ROWS)
        parts = []
        for v, here in [(from_doc[j * 40:(j + 1) * 40, cols], rd // 4 == x) for j in range(4)] + [
                (from_leaf[:, cols], rl // 16 == x), (from_suffix[:, cols], row // 64 == x)]:
            parts.append((v[:32], jnp.where(here, v[32:33] + v[33:34], NEG), jnp.where(here, 1.0, 0.0)))
        accum, top, total = merged(parts)
        for half in range(2):
            xs[b * 2 + half] = jnp.concatenate(
                [accum[half * 16:half * 16 + 16], top, total, jnp.zeros((6, ROWS), F32)], axis=0)

    for o in (2, 1, 3):
        push(xs.at[(x + o) % NX], xr.at[x], b_xs.at[o], b_xr.at[o], at_xz(x + o, z), head)
    xr[x] = xs[x]
    for o in (1, 3, 2):
        block = xr.at[(x - o) % NX]
        remote(block, block, b_xs.at[o], b_xr.at[o], pos, head).wait_recv()
    parts = []
    for i in range(NX):
        v = xr[i]
        parts.append((v[:16], v[16:17], v[17:18]))
    accum, _, total = merged(parts)

    at[z] = (accum / total).astype(BF16)
    for o in Z_FAR:
        push(at.at[z], at.at[z], c_zs.at[16 - o], c_zr.at[16 - o], at_xz(x, z + o), head)
    for o in (1, 3, 2):
        block = wx.at[(x - o) % NX]
        remote(block, block, w_s.at[o], w_r.at[o], pos, head).wait_recv()
    for r in Z_NEAR:
        block = at.at[(z + r) % NZ]
        remote(block, block, c_zs.at[r], c_zr.at[r], pos, head).wait_recv()

    eye = onehot(iota((ROWS, ROWS), 0) == iota((ROWS, ROWS), 1))
    attention = dot_nt(eye, at[...].reshape(ROWS, ROWS)).astype(BF16)
    for i in (2, 1, 3, 0):
        to = (x + i) % NX
        share = dot(attention, wx[to].reshape(2 * HD, HD)).astype(BF16)
        for n in range(NH):
            ob[to, n] = share[n * 32:(n + 1) * 32]
        for o in (4, 3, 5, 2, 6, 1, 7, 0):
            if i or o:
                n = (head + o) % NH
                push(ob.at[to, n], db.at[x, head], d_s.at[i * 8 + o], d_r.at[i * 8 + o], at_xz(to, z), n)
    db[x, head] = ob[x, head]
    for i in (1, 3, 2, 0):
        for o in range(NH):
            if i or o:
                block = db.at[(x - i) % NX, (head - o) % NH]
                remote(block, block, d_s.at[i * 8 + o], d_r.at[i * 8 + o], pos, head).wait_recv()
    out_ref[...] = jnp.sum(db[...].reshape(NX * NH, 32, HD).astype(F32), axis=0).astype(BF16)
    for c in sends:
        c.wait_send()


def per_device(queries, doc_kv, leaf_kv, suffix_kv, suffix_len, parent, row_leaf, out_weight):
    vmem = pl.BlockSpec(memory_space=pltpu.VMEM)
    smem = pl.BlockSpec(memory_space=pltpu.SMEM)
    hbm = pl.BlockSpec(memory_space=pl.ANY)
    dma = pltpu.SemaphoreType.DMA
    return pl.pallas_call(
        kernel,
        out_shape=jax.ShapeDtypeStruct((32, 128), BF16),
        in_specs=[hbm, smem, hbm, hbm, hbm, hbm, hbm, hbm],
        out_specs=vmem,
        scratch_shapes=[
            pltpu.VMEM((4, 1024), BF16),
            pltpu.VMEM((1, 64), I32),
            pltpu.VMEM((1, 256), I32),
            pltpu.VMEM((2, 2048, HD), BF16),
            pltpu.VMEM((2, 1024, HD), BF16),
            pltpu.VMEM((2, 4, 512, HD), BF16),
            pltpu.VMEM((4, 2, 4, 2, 16, HD), BF16),
            pltpu.VMEM((HD, 2048), BF16),
            pltpu.VMEM((HD, 1024), BF16),
            pltpu.VMEM((HD, 2048), BF16),
            pltpu.VMEM((NX, 4, 4, 16, HD), BF16),
            pltpu.VMEM((64, 32, HD), BF16),
            pltpu.VMEM((NX, 256, 256), BF16),
            pltpu.VMEM((512, 512), BF16),
            pltpu.VMEM((512, 512), BF16),
            pltpu.VMEM((128, 512), BF16),
            pltpu.VMEM((16, 16, 128), BF16),
            pltpu.VMEM((16, 16, 128), BF16),
            pltpu.VMEM((16, 32, 128), BF16),
            pltpu.VMEM((16, 32, 128), BF16),
            pltpu.VMEM((4, 24, ROWS), F32),
            pltpu.VMEM((4, 24, ROWS), F32),
            pltpu.VMEM((16, 16, ROWS), BF16),
            pltpu.VMEM((NX, NH, 32, HD), BF16),
            pltpu.VMEM((NX, NH, 32, HD), BF16),
            dma((7,)),
            dma((16,)), dma((16,)), dma((64,)), dma((64,)),
            dma((16,)), dma((16,)),
            dma((16,)), dma((16,)), dma((4,)), dma((4,)),
            dma((16,)), dma((16,)), dma((4,)), dma((4,)),
            dma((32,)), dma((32,)),
        ],
        compiler_params=pltpu.CompilerParams(
            collective_id=0, has_side_effects=True, vmem_limit_bytes=62 << 20),
        name="tree_attention",
    )(queries, suffix_len, parent.reshape(1, -1), row_leaf.reshape(1, -1), doc_kv, leaf_kv, suffix_kv,
      out_weight.reshape(4, 2, 4, 2, 16, HD))


def solution(mesh):
    in_specs = (
        P("seq", "head"),
        P(None, "seq", "head"),
        P(None, "seq", "head"),
        P(None, "seq", None, "head"),
        P("seq"),
        P(),
        P(),
        P("head", "seq"),
    )
    return jax.shard_map(
        per_device, mesh=mesh, in_specs=in_specs, out_specs=P("head", "seq"), check_vma=False)
```

```python
import jax
import jax.numpy as jnp
from jax import lax
from jax.experimental import pallas as pl
from jax.experimental.pallas import tpu as pltpu
from jax.sharding import PartitionSpec as P

MESH = pl.DeviceIdType.MESH
F32 = jnp.float32
BF16 = jnp.bfloat16
I32 = jnp.int32
NEG = -2.0 ** 100
NX, NZ, NH = 4, 16, 8
HD = 128
G = 8
ROWS = 256
DOC_SLOTS = 48
LEAF_SLOTS = 12
RATE = HD ** -0.5 * 1.4426950408889634
LEAF_AT = G // 2 * DOC_SLOTS
NT = (((1,), (1,)), ((), ()))
Z_FAR = (8, 7, 9, 6, 10, 5, 11, 4, 12, 3, 13, 2, 14, 1, 15)
Z_NEAR = Z_FAR[::-1]
Z_STEP = (1, 15, 2, 14, 3, 13, 4, 12)


def iota(shape, dim):
    return lax.broadcasted_iota(I32, shape, dim)


def dot(a, b):
    return jnp.dot(a, b, preferred_element_type=F32)


def dot_nt(a, b):
    return lax.dot_general(a, b, NT, preferred_element_type=F32)


def onehot(cond):
    return jnp.where(cond, 1.0, 0.0).astype(BF16)


def merged(parts):
    top = parts[0][1]
    for _, m, _ in parts[1:]:
        top = jnp.maximum(top, m)
    accum, total = None, None
    for a, m, l in parts:
        weight = jnp.exp2((m - top) * RATE)
        accum = a * weight if accum is None else accum + a * weight
        total = l * weight if total is None else total + l * weight
    return accum, top, total


def attend(scores_of, chunks, chunk, vt_ref):
    parts = []
    for c in range(chunks):
        s = scores_of(c)
        top = jnp.max(s, axis=0, keepdims=True)
        p = jnp.exp2(s * RATE - top * RATE)
        accum = dot(vt_ref[:, c * chunk:(c + 1) * chunk], p.astype(BF16))
        parts.append((accum, top, jnp.sum(p, axis=0, keepdims=True)))
    accum, top, total = merged(parts)
    level = top + jnp.log2(total) * (1 / RATE)
    high = level.astype(BF16).astype(F32)
    return accum / total, high, level - high


def turn(v, lanes):
    return pltpu.roll(v, lanes % 128, 1) if lanes % 128 else v


def kernel(q_hbm, len_ref, parent_hbm, rl_hbm, doc_hbm, leaf_hbm, suf_hbm, w_hbm, out_ref,
           q_ref, parent_ref, rl_ref, doc, leaf, suf, wv, doc_vt, leaf_vt, suf_vt, wx, qa, oh, ed, el, es, sl, rl_in, sb, rb, xs, xr, at, ob, db,
           ld, a_zs, a_zr, a_xs, a_xr, l_zs, l_zr, b_zs, b_zr, b_xs, b_xr, c_zs, c_zr, w_s, w_r, d_s, d_r):
    pos = lax.axis_index("seq")
    head = lax.axis_index("head")
    x, z = pos // NZ, pos % NZ
    quad = z // 4

    def at_xz(xx, zz):
        return (xx % NX) * NZ + zz % NZ

    def remote(src, dst, send, recv, seq_id, head_id):
        return pltpu.make_async_remote_copy(
            src_ref=src, dst_ref=dst, send_sem=send, recv_sem=recv,
            device_id=(seq_id, head_id), device_id_type=MESH)

    loads = [pltpu.make_async_copy(h, v, ld.at[i])
             for i, (h, v) in enumerate((
                 (suf_hbm, suf), (doc_hbm, doc), (leaf_hbm, leaf), (w_hbm, wv), (q_hbm, q_ref),
                 (parent_hbm, parent_ref), (rl_hbm, rl_ref)))]
    for i in (4, 5, 6, 0, 1, 2, 3):
        loads[i].start()

    barrier = pltpu.get_barrier_semaphore()
    for o in Z_STEP:
        pl.semaphore_signal(barrier, inc=1, device_id=(at_xz(x, z + o), head), device_id_type=MESH)
    for i in range(NX):
        for o in range(NH):
            if i or o:
                pl.semaphore_signal(
                    barrier, inc=1, device_id=(at_xz(x + i, z), (head + o) % NH), device_id_type=MESH)

    loads[4].wait()
    qf = q_ref[...].astype(F32)
    qa[pos] = jnp.concatenate([qf[:, g * HD:(g + 1) * HD] for g in range(G)], axis=0).astype(BF16)

    eye = onehot(iota((HD, HD), 0) == iota((HD, HD), 1))
    loads[5].wait()
    loads[6].wait()
    rl = rl_ref[...]
    leaf_hot = onehot(iota((64, ROWS), 0) == rl)
    parents = jnp.broadcast_to(parent_ref[...].astype(F32), (16, 64)).astype(BF16)
    rd = dot(parents, leaf_hot)[:1].astype(I32)
    before = onehot(iota((ROWS, ROWS), 0) < iota((ROWS, ROWS), 1))
    leaf_slot = jnp.sum(leaf_hot.astype(F32) * dot(leaf_hot, before), axis=0, keepdims=True).astype(I32)
    doc_hot = onehot(iota((16, ROWS), 0) == rd)
    doc_slot = jnp.sum(doc_hot.astype(F32) * dot(doc_hot, before), axis=0, keepdims=True).astype(I32)
    row = iota((1, ROWS), 1)

    my_doc = x * 4 + quad
    want = jnp.concatenate([
        jnp.where(rd == my_doc, doc_slot, 128),
        jnp.where(rl == pos, leaf_slot, 128),
        jnp.full((14, ROWS), 128, I32),
    ], axis=0).astype(F32).astype(BF16)
    for t in range(NX):
        lane = iota((ROWS, 256), 1)
        spread = onehot(iota((ROWS, 256), 0) == t * 64 + (lane // 16) * 4 + lane % 4)
        wide = dot(want, spread).astype(I32)
        a = (iota((1, 256), 1) // 4) % 4
        first = jnp.where(wide[0:1] < 128, wide[0:1] + a * DOC_SLOTS, -1)
        second = jnp.where(wide[1:2] < 128, wide[1:2] + (LEAF_AT + a * LEAF_SLOTS), -1)
        sub = iota((256, 256), 0)
        oh[t] = onehot((sub == first) | (sub == second))

    pl.semaphore_wait(barrier, len(Z_STEP) + NX * NH - 1)

    sends = []

    def push(src, dst, send, recv, seq_id, head_id):
        c = remote(src, dst, send, recv, seq_id, head_id)
        c.start()
        sends.append(c)

    def sent():
        for c in sends:
            c.wait_send()
        sends.clear()

    for o in Z_STEP:
        push(qa.at[pos], qa.at[pos], a_zs.at[16 - o], a_zr.at[16 - o], at_xz(x, z + o), head)
    for r in (0, 1, 15, 2, 14, 3, 13, 4, 12, 5, 11, 6, 10, 7, 9, 8):
        block = qa.at[at_xz(x, z + r)]
        if r:
            remote(block, block, a_zs.at[r], a_zr.at[r], pos, head).wait_recv()
        if 1 <= r <= 4:
            push(block, block, a_zs.at[r + 4], a_zr.at[r + 4], at_xz(x, z - 4), head)
        if 13 <= r <= 15:
            push(block, block, a_zs.at[r - 4], a_zr.at[r - 4], at_xz(x, z + 4), head)
        for i in (1, 3, 2):
            push(block, block, a_xs.at[i * 16 + r], a_xr.at[i * 16 + r], at_xz(x + i, z), head)

    loads[0].wait()
    for i in range(4):
        suf_vt[:, i * 512:(i + 1) * 512] = dot_nt(eye, suf[1, i]).astype(BF16)
    own_q = jnp.concatenate([qa[pos].astype(F32), jnp.zeros((96, HD), F32)], axis=0).astype(BF16)
    lane4 = iota((1, 128), 1) % 4
    live = jnp.where(lane4 == 0, len_ref[0], jnp.where(lane4 == 1, len_ref[1], jnp.where(
        lane4 == 2, len_ref[2], len_ref[3])))

    def suffix_scores(c):
        s = dot_nt(suf[0, c], own_q)
        return jnp.where((lane4 == c) & (iota((512, 128), 0) < live), s, NEG)

    accum, high, low = attend(suffix_scores, 4, 512, suf_vt)

    def send_parts(out, into, send, recv, pair):
        def start(c):
            to = pair * 4 + (z + c) % 4
            remote(out.at[to], into.at[z], send.at[to], recv.at[z], at_xz(x, to), head).start()

        @pl.when(z // 4 == pair)
        def _():
            for c in (1, 2, 3):
                start(c)

        @pl.when(z // 4 != pair)
        def _():
            for c in range(4):
                start(c)

    lane = iota((1, 128), 1)
    stat = jnp.concatenate([high, low, jnp.zeros((14, 128), F32)], axis=0)
    for pair in range(4):
        a0, a1, v = turn(accum, -8 * pair), turn(accum, 8 - 8 * pair), turn(stat, 16 - 8 * pair)
        for c in range(4):
            sl[pair * 4 + c] = jnp.where(lane < 8, a0[c * 32:c * 32 + 16], jnp.where(
                lane < 16, a1[c * 32 + 16:c * 32 + 32], v)).astype(BF16)
        send_parts(sl, rl_in, l_zs, l_zr, pair)

    loads[1].wait()
    for c in range(4):
        doc_vt[:, c * 512:(c + 1) * 512] = dot_nt(eye, doc[1, c * 512:(c + 1) * 512, :]).astype(BF16)
    loads[2].wait()
    for c in range(2):
        leaf_vt[:, c * 512:(c + 1) * 512] = dot_nt(eye, leaf[1, c * 512:(c + 1) * 512, :]).astype(BF16)
    halves = [None, None]
    for i in (0, 1, 3, 2):
        plane = (x - i) % NX
        if i:
            for r in range(16):
                block = qa.at[at_xz(plane, z + r)]
                remote(block, block, a_xs.at[i * 16 + r], a_xr.at[i * 16 + r], pos, head).wait_recv()
        got = qa[pl.ds(plane * NZ, NZ)]
        for hq in range(2):
            more = dot(oh[plane], got[:, hq * 16:(hq + 1) * 16].reshape(256, HD))
            halves[hq] = more if halves[hq] is None else halves[hq] + more
    halves = [v.astype(BF16) for v in halves]
    rest = jnp.zeros((32, HD), BF16)

    mine = jnp.concatenate([halves[0][LEAF_AT:LEAF_AT + 48], halves[1][LEAF_AT:LEAF_AT + 48], rest], axis=0)
    accum, high, low = attend(lambda c: dot_nt(leaf[0, c * 512:(c + 1) * 512, :], mine), 2, 512, leaf_vt)
    packed = jnp.concatenate([accum, high, low, jnp.zeros((14, 128), F32)], axis=0).astype(BF16)
    source = iota((128, 512), 0)
    place = iota((128, 512), 1)
    leaf_part = dot(packed, onehot(
        (place % 128 >= 96) & (place % 128 < 120) & (source == (place // 128) * 24 + place % 128 - 96)))

    spread = iota((16, 128), 0) == iota((16, 128), 1) // 8
    spread = spread & (iota((16, 128), 1) < 120)
    gather = onehot((iota((128, 128), 1) >= 120) & (iota((128, 128), 0) % 8 == iota((128, 128), 1) - 120))
    for pair in range(4):
        mine = jnp.concatenate([halves[pair // 2][(pair % 2) * 96:(pair % 2) * 96 + 96], rest], axis=0)
        accum, high, low = attend(lambda c: dot_nt(doc[0, c * 512:(c + 1) * 512, :], mine), 4, 512, doc_vt)
        other = leaf_part[:, pair * 128:(pair + 1) * 128]
        accum = jnp.where(lane < 96, accum, other[:HD])
        high = jnp.where(lane < 96, high, other[HD:HD + 1])
        low = jnp.where(lane < 96, low, other[HD + 1:HD + 2])
        both = jnp.concatenate([jnp.where(spread, high, 0.0), jnp.where(spread, low, 0.0)], axis=0).astype(BF16)
        both = dot(both, gather)
        for c in range(4):
            sb[pair * 4 + c] = jnp.where(lane < 120, accum[c * 32:(c + 1) * 32], both).astype(BF16)
        send_parts(sb, rb, b_zs, b_zr, pair)

    sent()

    loads[3].wait()
    for o in (2, 1, 3):
        to = (x + o) % NX
        push(wv.at[:, to // 2, :, to % 2], wx.at[x], w_s.at[o], w_r.at[o], at_xz(x + o, z), head)
    wx[x] = wv[:, x // 2, :, x % 2]

    sub = iota((512, ROWS), 0)
    for b in range(2):
        cols = slice(b * ROWS, (b + 1) * ROWS)
        ed[:, cols] = onehot(sub == jnp.where(rd // 4 == x, (rd % 4) * 128 + b * DOC_SLOTS + doc_slot, -1))
        el[:, cols] = onehot(sub == jnp.where(
            rl // 16 == x, (rl % 4) * 128 + (rl // 4) % 4 * 32 + b * LEAF_SLOTS + leaf_slot, -1))
        es[:, cols] = onehot(sub[:128] == jnp.where(row // 64 == x, (row // 4) % 16 * 8 + b * 4 + row % 4, -1))

    def take(out, into, send, recv):
        into[z] = out[z]
        for o in Z_NEAR:
            i = (z - o) % NZ
            c = remote(out.at[i], into.at[i], send.at[i], recv.at[i], pos, head)
            c.wait_send()
            c.wait_recv()

    take(sl, rl_in, l_zs, l_zr)
    got = [rl_in[i].astype(F32) for i in range(16)]

    def collect(first, rows):
        v = jnp.zeros((rows, 128), F32)
        for i in range(16):
            v = jnp.where(lane // 8 == i, turn(got[i][:rows], 8 * i - first), v)
        return v

    left = jnp.concatenate([collect(0, 16), collect(8, 16), collect(16, 8)], axis=0).astype(BF16)
    from_suffix = dot(left, es[...])

    take(sb, rb, b_zs, b_zr)
    scatter = onehot((iota((128, 128), 0) >= 120) & (iota((128, 128), 0) - 120 == iota((128, 128), 1) % 8))
    stats = dot(rb[...].reshape(512, 128), scatter)
    gap = jnp.zeros((6, 128), F32)
    got = []
    for i in range(16):
        high = jnp.sum(jnp.where(spread, stats[i * 32:i * 32 + 16], 0.0), axis=0, keepdims=True)
        low = jnp.sum(jnp.where(spread, stats[i * 32 + 16:i * 32 + 32], 0.0), axis=0, keepdims=True)
        got.append(jnp.concatenate([rb[i].astype(F32), high, low, gap], axis=0))
    left, leaves = [], []
    for j in range(4):
        left.append(jnp.concatenate([got[4 * k + j] for k in range(4)], axis=1))
        v = turn(got[j], 32)
        for k in range(1, 4):
            v = jnp.where(lane // 32 == k, turn(got[4 * k + j], 32 + 32 * k), v)
        leaves.append(v)
    from_leaf = dot(jnp.concatenate(leaves, axis=1).astype(BF16), el[...])
    from_doc = dot(jnp.concatenate(left, axis=0).astype(BF16), ed[...])

    for b in range(2):
        cols = slice(b * ROWS, (b + 1) * ROWS)
        parts = []
        for v, here in [(from_doc[j * 40:(j + 1) * 40, cols], rd // 4 == x) for j in range(4)] + [
                (from_leaf[:, cols], rl // 16 == x), (from_suffix[:, cols], row // 64 == x)]:
            parts.append((v[:32], jnp.where(here, v[32:33] + v[33:34], NEG), jnp.where(here, 1.0, 0.0)))
        accum, top, total = merged(parts)
        for half in range(2):
            xs[b * 2 + half] = jnp.concatenate(
                [accum[half * 16:half * 16 + 16], top, total, jnp.zeros((6, ROWS), F32)], axis=0)

    for o in (2, 1, 3):
        push(xs.at[(x + o) % NX], xr.at[x], b_xs.at[o], b_xr.at[o], at_xz(x + o, z), head)
    xr[x] = xs[x]
    for o in (1, 3, 2):
        block = xr.at[(x - o) % NX]
        remote(block, block, b_xs.at[o], b_xr.at[o], pos, head).wait_recv()
    parts = []
    for i in range(NX):
        v = xr[i]
        parts.append((v[:16], v[16:17], v[17:18]))
    accum, _, total = merged(parts)

    at[z] = (accum / total).astype(BF16)
    before_z = list(sends)
    sends.clear()
    for o in Z_FAR:
        push(at.at[z], at.at[z], c_zs.at[16 - o], c_zr.at[16 - o], at_xz(x, z + o), head)
    for c in before_z:
        c.wait_send()
    for o in (1, 3, 2):
        block = wx.at[(x - o) % NX]
        remote(block, block, w_s.at[o], w_r.at[o], pos, head).wait_recv()
    for r in Z_NEAR:
        block = at.at[(z + r) % NZ]
        remote(block, block, c_zs.at[r], c_zr.at[r], pos, head).wait_recv()

    eye = onehot(iota((ROWS, ROWS), 0) == iota((ROWS, ROWS), 1))
    attention = dot_nt(eye, at[...].reshape(ROWS, ROWS)).astype(BF16)
    for i in (2, 1, 3, 0):
        to = (x + i) % NX
        share = dot(attention, wx[to].reshape(2 * HD, HD)).astype(BF16)
        for n in range(NH):
            ob[to, n] = share[n * 32:(n + 1) * 32]
        for o in (4, 3, 5, 2, 6, 1, 7, 0):
            if i or o:
                n = (head + o) % NH
                push(ob.at[to, n], db.at[x, head], d_s.at[i * 8 + o], d_r.at[i * 8 + o], at_xz(to, z), n)
    db[x, head] = ob[x, head]
    sent()
    for i in (1, 3, 2, 0):
        for o in range(NH):
            if i or o:
                block = db.at[(x - i) % NX, (head - o) % NH]
                remote(block, block, d_s.at[i * 8 + o], d_r.at[i * 8 + o], pos, head).wait_recv()
    out_ref[...] = jnp.sum(db[...].reshape(NX * NH, 32, HD).astype(F32), axis=0).astype(BF16)


def per_device(queries, doc_kv, leaf_kv, suffix_kv, suffix_len, parent, row_leaf, out_weight):
    vmem = pl.BlockSpec(memory_space=pltpu.VMEM)
    smem = pl.BlockSpec(memory_space=pltpu.SMEM)
    hbm = pl.BlockSpec(memory_space=pl.ANY)
    dma = pltpu.SemaphoreType.DMA
    return pl.pallas_call(
        kernel,
        out_shape=jax.ShapeDtypeStruct((32, 128), BF16),
        in_specs=[hbm, smem, hbm, hbm, hbm, hbm, hbm, hbm],
        out_specs=vmem,
        scratch_shapes=[
            pltpu.VMEM((4, 1024), BF16),
            pltpu.VMEM((1, 64), I32),
            pltpu.VMEM((1, 256), I32),
            pltpu.VMEM((2, 2048, HD), BF16),
            pltpu.VMEM((2, 1024, HD), BF16),
            pltpu.VMEM((2, 4, 512, HD), BF16),
            pltpu.VMEM((4, 2, 4, 2, 16, HD), BF16),
            pltpu.VMEM((HD, 2048), BF16),
            pltpu.VMEM((HD, 1024), BF16),
            pltpu.VMEM((HD, 2048), BF16),
            pltpu.VMEM((NX, 4, 4, 16, HD), BF16),
            pltpu.VMEM((64, 32, HD), BF16),
            pltpu.VMEM((NX, 256, 256), BF16),
            pltpu.VMEM((512, 512), BF16),
            pltpu.VMEM((512, 512), BF16),
            pltpu.VMEM((128, 512), BF16),
            pltpu.VMEM((16, 16, 128), BF16),
            pltpu.VMEM((16, 16, 128), BF16),
            pltpu.VMEM((16, 32, 128), BF16),
            pltpu.VMEM((16, 32, 128), BF16),
            pltpu.VMEM((4, 24, ROWS), F32),
            pltpu.VMEM((4, 24, ROWS), F32),
            pltpu.VMEM((16, 16, ROWS), BF16),
            pltpu.VMEM((NX, NH, 32, HD), BF16),
            pltpu.VMEM((NX, NH, 32, HD), BF16),
            dma((7,)),
            dma((16,)), dma((16,)), dma((64,)), dma((64,)),
            dma((16,)), dma((16,)),
            dma((16,)), dma((16,)), dma((4,)), dma((4,)),
            dma((16,)), dma((16,)), dma((4,)), dma((4,)),
            dma((32,)), dma((32,)),
        ],
        compiler_params=pltpu.CompilerParams(
            collective_id=0, has_side_effects=True, vmem_limit_bytes=62 << 20),
        name="tree_attention",
    )(queries, suffix_len, parent.reshape(1, -1), row_leaf.reshape(1, -1), doc_kv, leaf_kv, suffix_kv,
      out_weight.reshape(4, 2, 4, 2, 16, HD))


def solution(mesh):
    in_specs = (
        P("seq", "head"),
        P(None, "seq", "head"),
        P(None, "seq", "head"),
        P(None, "seq", None, "head"),
        P("seq"),
        P(),
        P(),
        P("head", "seq"),
    )
    return jax.shard_map(
        per_device, mesh=mesh, in_specs=in_specs, out_specs=P("head", "seq"), check_vma=False)
```
